32 devices in a mesh: row: 8 (over z, x), col: 2 (over core), ka: 2 (over y).
Axes of the slice: x: 2, y: 2, z: 4, core: 2. Of those that a mesh axis runs over, the one named last changes fastest.
Arguments:
- density_rows: bfloat16 [1024, 1024], P('row'), may hold values from -0.1 to 0.9
- response_start: bfloat16 [1024, 1024], P(None, ('col', 'ka')), may hold values from -6 to 6
- density_pattern: int32 [16, 8], replicated, may hold values from 0 to 15
- response_pattern: int32 [16, 8], replicated, may hold values from 0 to 15
Outputs:
- response: bfloat16 [1024, 1024], P('row', ('col', 'ka'))
The draws below stay inside these ranges and needn't reach their ends.
Inputs may be any that keep to these rules, and one draw needn't show every extreme that they name: `density_pattern`: repeats may occur within a block row. `response_pattern`: repeats may occur within a block row.
All inputs are finite; a program needn't handle non-finite values.
Results may differ from the reference program's by a relative error of at most 0.017.
Values may be sent and summed in bfloat16 or wider, within the bound.
A program may use at most 64 MiB of HBM per device.

```python
import math
import jax
import jax.numpy as jnp
from jax import lax

BLOCK = 64
KB = 8
ITERS = 2
NBLOCKS = 16
ORDER = 1024


def draw_density_rows(key, part):
    key = jax.random.fold_in(key, 11)
    noise_key, diag_key = jax.random.split(key)
    row_ids = lax.broadcasted_iota(jnp.int32, (ORDER, ORDER), 0)
    col_ids = lax.broadcasted_iota(jnp.int32, (ORDER, ORDER), 1)
    spread = 0.4 / math.sqrt(BLOCK * (KB + 1))
    noise = spread * jax.random.normal(noise_key, (ORDER, ORDER), jnp.float32)
    diagonal = jax.random.uniform(diag_key, (ORDER, ORDER), jnp.float32, 0.2, 0.8)
    noise = jnp.clip(noise, -0.09, 0.09)
    return jnp.where(row_ids == col_ids, diagonal, noise).astype(jnp.bfloat16)


def set_ends(array, rng, low, high):
    longest = array.shape.index(max(array.shape))
    spots = []
    for shift in (0, 1):
        where = [jax.random.randint(jax.random.fold_in(rng, axis), (), 0, length) for axis, length in enumerate(array.shape)]
        where[longest] = (where[longest] + shift) % array.shape[longest]
        spots.append(tuple(where))
    return array.at[spots[0]].set(low).at[spots[1]].set(high)


def shard_levels(stream_key, extent, cuts, smallest, high):
    def one(axis_at, shards_of):
        draws = jax.random.uniform(jax.random.fold_in(jax.random.fold_in(stream_key, 6), axis_at), (shards_of,), jnp.float32, smallest / len(cuts), high / len(cuts))
        return jnp.repeat(jnp.exp(draws), extent[axis_at] // shards_of).reshape((-1,) + (1,) * (len(extent) - axis_at - 1))

    level = one(*cuts[0])
    for cut in cuts[1:]:
        level = level * one(*cut)
    return level


def centred(stream_key, shape, width, reach, pieces=(), held_as=jnp.bfloat16):
    drawn = jax.random.normal(stream_key, shape, jnp.float32) * width
    if len(pieces) > 0:
        drawn = shard_levels(stream_key, shape, pieces, -0.22, 0.18) * drawn
    return jnp.clip(drawn, min=-reach, max=reach).astype(held_as)


def setup_inputs(seed: int = 0) -> dict:
    streams_of = jax.random.split(jax.random.key(seed), 5)
    return {
        "density_rows": draw_density_rows(jax.random.fold_in(streams_of[4], 71), 0),
        "response_start": centred(streams_of[1], (ORDER, ORDER), 1.0, 6.0, ((1, 4),)),
        "density_pattern": set_ends(jax.random.randint(streams_of[2], (NBLOCKS, KB), 0, NBLOCKS), jax.random.fold_in(streams_of[2], 1), 0, NBLOCKS - 1).astype(jnp.int32),
        "response_pattern": set_ends(jax.random.randint(streams_of[3], (NBLOCKS, KB), 0, NBLOCKS), jax.random.fold_in(streams_of[3], 1), 0, NBLOCKS - 1).astype(jnp.int32),
    }


def block_mask(pattern_list, blocks):
    row_ids = lax.broadcasted_iota(jnp.int32, (blocks, blocks), 0)
    col_ids = lax.broadcasted_iota(jnp.int32, (blocks, blocks), 1)
    listed = jnp.any(pattern_list[:, None, :] == col_ids[:, :, None], axis=2)
    return jnp.logical_or(listed, row_ids == col_ids)


def expand(mask_part, block_width):
    return jnp.repeat(jnp.repeat(mask_part, block_width, axis=0), block_width, axis=1)


def reference(density_rows, response_start, density_pattern, response_pattern):
    keep_density = expand(block_mask(density_pattern, NBLOCKS), BLOCK)
    keep_response = expand(block_mask(response_pattern, NBLOCKS), BLOCK)
    density = jnp.where(keep_density, density_rows, jnp.zeros_like(density_rows))
    current = jnp.where(keep_response, response_start, jnp.zeros_like(response_start))
    for iteration in range(ITERS):
        forward = jnp.dot(density, current, preferred_element_type=jnp.float32)
        backward = jnp.dot(current, density, preferred_element_type=jnp.float32)
        sym = forward + backward
        qround = sym.astype(jnp.bfloat16)
        wround = forward.astype(jnp.bfloat16)
        second = jnp.dot(density, wround, preferred_element_type=jnp.float32)
        tail = jnp.dot(qround, density, preferred_element_type=jnp.float32)
        updated = jnp.where(keep_response, 3.0 * sym - 2.0 * (second + tail), jnp.zeros_like(sym))
        current = updated.astype(jnp.bfloat16)
    return current
```

```python
import functools

import jax
import jax.numpy as jnp
from jax import lax
from jax.experimental import pallas as pl
from jax.experimental.pallas import tpu as pltpu
from jax.sharding import PartitionSpec as P

BLOCK = 64
ITERS = 2
LANES = 2
MESH = pl.DeviceIdType.MESH


def keep_row(pattern_ref, block_row, first_col, cols):
    listed = pattern_ref[pl.ds(block_row, 1), :]
    col_block = (lax.broadcasted_iota(jnp.int32, (1, cols), 1) + first_col) // BLOCK
    keep = col_block == block_row
    for k in range(listed.shape[1]):
        keep = jnp.logical_or(keep, col_block == listed[:, k : k + 1])
    return keep


def masked(keep, values):
    values = values.astype(jnp.float32)
    return jnp.where(jnp.broadcast_to(keep, values.shape), values, jnp.zeros_like(values))


def dot(a, b):
    return jnp.dot(a, b, preferred_element_type=jnp.float32)


def kernel(
    axes,
    nrow,
    ncol,
    nka,
    density_in,
    start_in,
    dpat,
    rpat,
    out_ref,
    density,
    start,
    fwd,
    sym,
    cols_of,
    rows_of,
    row_send,
    row_recv,
    share_send,
    share_recv,
):
    rows, order = density_in.shape
    share_cols = start_in.shape[1]
    nshare = ncol * nka
    nhi = nrow // LANES
    per_row = rows // BLOCK
    row = lax.axis_index("row")
    col = lax.axis_index("col")
    ka = lax.axis_index("ka")
    share = col * nka + ka
    hi, lo = row // LANES, row % LANES

    def device(r, c, k):
        where = {"row": r, "col": c, "ka": k}
        return tuple(where[name] for name in axes)

    hi_peers = [((hi + d) % nhi) * LANES + lo for d in range(1, nhi)]
    lo_peers = [hi * LANES + (lo + d) % LANES for d in range(1, LANES)]
    share_peers = [(share + d) % nshare for d in range(1, nshare)]

    def own_rows(r):
        return pl.ds(pl.multiple_of(r * rows, rows), rows)

    def row_copy(a, slot, target, sem):
        return pltpu.make_async_remote_copy(
            src_ref=cols_of.at[a, own_rows(slot), :],
            dst_ref=cols_of.at[a, own_rows(slot), :],
            send_sem=row_send.at[a, sem],
            recv_sem=row_recv.at[a, slot],
            device_id=device(target, col, ka),
            device_id_type=MESH,
        )

    def row_start(a):
        started = []
        for i, peer in enumerate(hi_peers + lo_peers):
            copy = row_copy(a, row, peer, i)
            copy.start()
            started.append(copy)
        return started

    def row_relay(a, started):
        sem = len(started)
        for peer in hi_peers:
            row_copy(a, peer, peer, 0).wait_recv()
            for target in lo_peers:
                copy = row_copy(a, peer, target, sem)
                copy.start()
                started.append(copy)
                sem += 1

    def row_finish(a):
        for d in range(nhi):
            for e in range(1, LANES):
                slot = ((hi + d) % nhi) * LANES + (lo + e) % LANES
                row_copy(a, slot, slot, 0).wait_recv()

    def share_copy(a, slot, target, sem):
        return pltpu.make_async_remote_copy(
            src_ref=rows_of.at[a, slot],
            dst_ref=rows_of.at[a, slot],
            send_sem=share_send.at[a, sem],
            recv_sem=share_recv.at[a, slot],
            device_id=device(row, target // nka, target % nka),
            device_id_type=MESH,
        )

    def share_start(a):
        started = []
        for i, peer in enumerate(share_peers):
            copy = share_copy(a, share, peer, i)
            copy.start()
            started.append(copy)
        return started

    def share_finish(a):
        for peer in share_peers:
            share_copy(a, peer, peer, 0).wait_recv()

    def left(a):
        return dot(density[...], cols_of[a])

    def right(a):
        total = None
        for s in range(nshare):
            part = dot(rows_of[a, s], cols_of[0, s * share_cols : (s + 1) * share_cols, :])
            total = part if total is None else total + part
        return total

    barrier = pltpu.get_barrier_semaphore()
    greeted = [device(r, col, ka) for r in hi_peers + lo_peers]
    greeted += [device(row, s // nka, s % nka) for s in share_peers]
    for peer in greeted:
        pl.semaphore_signal(barrier, inc=1, device_id=peer, device_id_type=MESH)

    for i in range(per_row):
        keep = keep_row(dpat, row * per_row + i, 0, order)
        part = slice(i * BLOCK, (i + 1) * BLOCK)
        density[part, :] = masked(keep, density_in[part, :]).astype(jnp.bfloat16)
    share_first = pl.multiple_of(share * share_cols, share_cols)
    cols_of[0, own_rows(row), :] = density[:, pl.ds(share_first, share_cols)]
    pl.semaphore_wait(barrier, len(greeted))
    sent = row_start(0)

    for b in range(order // BLOCK):
        keep = keep_row(rpat, b, share_first, share_cols)
        part = slice(b * BLOCK, (b + 1) * BLOCK)
        start[part, :] = masked(keep, start_in[part, :]).astype(jnp.bfloat16)
    rows_of[0, share] = start[own_rows(row), :]
    sent += share_start(0)
    fwd[...] = dot(density[...], start[...])
    cols_of[1, own_rows(row), :] = fwd[...].astype(jnp.bfloat16)

    d_sent = sent[: nrow // LANES - 1 + LANES - 1]
    relayed = list(d_sent)
    row_relay(0, relayed)
    sent += relayed[len(d_sent) :]
    w_sent = row_start(1)
    row_finish(0)

    a_row, a_share = 1, 0
    for iteration in range(ITERS):
        share_finish(a_share)
        sym[...] = fwd[...] + right(a_share)
        rows_of[a_share + 1, share] = sym[...].astype(jnp.bfloat16)
        sent += share_start(a_share + 1)
        row_relay(a_row, w_sent)
        sent += w_sent
        row_finish(a_row)
        second = left(a_row)
        share_finish(a_share + 1)
        total = 3.0 * sym[...] - 2.0 * (second + right(a_share + 1))
        for i in range(per_row):
            keep = keep_row(rpat, row * per_row + i, share_first, share_cols)
            part = slice(i * BLOCK, (i + 1) * BLOCK)
            updated = masked(keep, total[part, :]).astype(jnp.bfloat16)
            if iteration == ITERS - 1:
                out_ref[part, :] = updated
            else:
                rows_of[a_share + 2, share, part, :] = updated
        if iteration == ITERS - 1:
            break
        a_row, a_share = a_row + 1, a_share + 2
        cols_of[a_row, own_rows(row), :] = rows_of[a_share, share]
        x_sent = row_start(a_row)
        sent += share_start(a_share)
        row_relay(a_row, x_sent)
        sent += x_sent
        row_finish(a_row)
        fwd[...] = left(a_row)
        a_row += 1
        cols_of[a_row, own_rows(row), :] = fwd[...].astype(jnp.bfloat16)
        w_sent = row_start(a_row)

    for copy in sent:
        copy.wait_send()


def solution(mesh):
    nrow, ncol, nka = (mesh.shape[name] for name in ("row", "col", "ka"))
    nshare = ncol * nka

    def body(density_rows, response_start, density_pattern, response_pattern):
        rows, order = density_rows.shape
        share_cols = response_start.shape[1]
        row_sends = nrow // LANES - 1 + LANES - 1 + (nrow // LANES - 1) * (LANES - 1)
        vmem = pl.BlockSpec(memory_space=pltpu.VMEM)
        return pl.pallas_call(
            functools.partial(kernel, mesh.axis_names, nrow, ncol, nka),
            out_shape=jax.ShapeDtypeStruct((rows, share_cols), jnp.bfloat16),
            in_specs=[vmem] * 4,
            out_specs=vmem,
            scratch_shapes=[
                pltpu.VMEM((rows, order), jnp.bfloat16),
                pltpu.VMEM((order, share_cols), jnp.bfloat16),
                pltpu.VMEM((rows, share_cols), jnp.float32),
                pltpu.VMEM((rows, share_cols), jnp.float32),
                pltpu.VMEM((2 * ITERS, order, share_cols), jnp.bfloat16),
                pltpu.VMEM((2 * ITERS, nshare, rows, share_cols), jnp.bfloat16),
                pltpu.SemaphoreType.DMA((2 * ITERS, row_sends)),
                pltpu.SemaphoreType.DMA((2 * ITERS, nrow)),
                pltpu.SemaphoreType.DMA((2 * ITERS, nshare)),
                pltpu.SemaphoreType.DMA((2 * ITERS, nshare)),
            ],
            compiler_params=pltpu.CompilerParams(
                collective_id=0, has_side_effects=True, vmem_limit_bytes=40 * 1024 * 1024
            ),
            cost_estimate=pl.CostEstimate(
                flops=8 * ITERS * rows * order * share_cols,
                bytes_accessed=2 * order * (rows + share_cols),
                transcendentals=0,
            ),
        )(density_rows, response_start, density_pattern, response_pattern)

    return jax.shard_map(
        body,
        mesh=mesh,
        in_specs=(P("row", None), P(None, ("col", "ka")), P(), P()),
        out_specs=P("row", ("col", "ka")),
        check_vma=False,
    )
```

```python
import functools

import jax
import jax.numpy as jnp
from jax import lax
from jax.experimental import pallas as pl
from jax.experimental.pallas import tpu as pltpu
from jax.sharding import PartitionSpec as P

BLOCK = 64
ITERS = 2
LANES = 2
MESH = pl.DeviceIdType.MESH


def keep_row(pattern_ref, block_row, first_col, cols):
    listed = pattern_ref[pl.ds(block_row, 1), :]
    col_block = (lax.broadcasted_iota(jnp.int32, (1, cols), 1) + first_col) // BLOCK
    keep = col_block == block_row
    for k in range(listed.shape[1]):
        keep = jnp.logical_or(keep, col_block == listed[:, k : k + 1])
    return keep


def masked(keep, values):
    values = values.astype(jnp.float32)
    return jnp.where(jnp.broadcast_to(keep, values.shape), values, jnp.zeros_like(values))


def dot(a, b):
    return jnp.dot(a, b, preferred_element_type=jnp.float32)


def kernel(
    axes,
    nrow,
    ncol,
    nka,
    density_in,
    start_in,
    dpat,
    rpat,
    out_ref,
    density,
    start,
    fwd,
    sym,
    cols_of,
    rows_of,
    row_send,
    row_recv,
    share_send,
    share_recv,
):
    rows, order = density_in.shape
    share_cols = start_in.shape[1]
    nshare = ncol * nka
    nhi = nrow // LANES
    per_row = rows // BLOCK
    row = lax.axis_index("row")
    col = lax.axis_index("col")
    ka = lax.axis_index("ka")
    share = col * nka + ka
    hi, lo = row // LANES, row % LANES

    def device(r, c, k):
        where = {"row": r, "col": c, "ka": k}
        return tuple(where[name] for name in axes)

    hi_peers = [((hi + d) % nhi) * LANES + lo for d in range(1, nhi)]
    lo_peers = [hi * LANES + (lo + d) % LANES for d in range(1, LANES)]
    share_peers = [(share + d) % nshare for d in range(1, nshare)]

    def own_rows(r):
        return pl.ds(pl.multiple_of(r * rows, rows), rows)

    def row_copy(a, slot, target, sem):
        return pltpu.make_async_remote_copy(
            src_ref=cols_of.at[a, own_rows(slot), :],
            dst_ref=cols_of.at[a, own_rows(slot), :],
            send_sem=row_send.at[a, sem],
            recv_sem=row_recv.at[a, slot],
            device_id=device(target, col, ka),
            device_id_type=MESH,
        )

    def row_start(a):
        started = []
        for i, peer in enumerate(hi_peers + lo_peers):
            copy = row_copy(a, row, peer, i)
            copy.start()
            started.append(copy)
        return started

    def row_relay(a, started):
        sem = len(started)
        for peer in hi_peers:
            row_copy(a, peer, peer, 0).wait_recv()
            for target in lo_peers:
                copy = row_copy(a, peer, target, sem)
                copy.start()
                started.append(copy)
                sem += 1

    def row_finish(a):
        for d in range(nhi):
            for e in range(1, LANES):
                slot = ((hi + d) % nhi) * LANES + (lo + e) % LANES
                row_copy(a, slot, slot, 0).wait_recv()

    def share_copy(a, slot, target, sem):
        return pltpu.make_async_remote_copy(
            src_ref=rows_of.at[a, slot],
            dst_ref=rows_of.at[a, slot],
            send_sem=share_send.at[a, sem],
            recv_sem=share_recv.at[a, slot],
            device_id=device(row, target // nka, target % nka),
            device_id_type=MESH,
        )

    def share_start(a):
        started = []
        for i, peer in enumerate(share_peers):
            copy = share_copy(a, share, peer, i)
            copy.start()
            started.append(copy)
        return started

    def share_finish(a):
        for peer in share_peers:
            share_copy(a, peer, peer, 0).wait_recv()

    def left(a):
        return dot(density[...], cols_of[a])

    def right(a):
        total = None
        for s in range(nshare):
            part = dot(rows_of[a, s], cols_of[0, s * share_cols : (s + 1) * share_cols, :])
            total = part if total is None else total + part
        return total

    barrier = pltpu.get_barrier_semaphore()
    greeted = [device(r, col, ka) for r in hi_peers + lo_peers]
    greeted += [device(row, s // nka, s % nka) for s in share_peers]
    for peer in greeted:
        pl.semaphore_signal(barrier, inc=1, device_id=peer, device_id_type=MESH)

    for i in range(per_row):
        keep = keep_row(dpat, row * per_row + i, 0, order)
        part = slice(i * BLOCK, (i + 1) * BLOCK)
        density[part, :] = masked(keep, density_in[part, :]).astype(jnp.bfloat16)
    share_first = pl.multiple_of(share * share_cols, share_cols)
    cols_of[0, own_rows(row), :] = density[:, pl.ds(share_first, share_cols)]
    pl.semaphore_wait(barrier, len(greeted))
    sent = row_start(0)

    for b in range(order // BLOCK):
        keep = keep_row(rpat, b, share_first, share_cols)
        part = slice(b * BLOCK, (b + 1) * BLOCK)
        start[part, :] = masked(keep, start_in[part, :]).astype(jnp.bfloat16)
    rows_of[0, share] = start[own_rows(row), :]
    sent += share_start(0)
    fwd[...] = dot(density[...], start[...])
    cols_of[1, own_rows(row), :] = fwd[...].astype(jnp.bfloat16)

    d_sent = sent[: nrow // LANES - 1 + LANES - 1]
    relayed = list(d_sent)
    row_relay(0, relayed)
    sent += relayed[len(d_sent) :]
    w_sent = row_start(1)
    row_finish(0)

    a_row, a_share = 1, 0
    for iteration in range(ITERS):
        share_finish(a_share)
        sym[...] = fwd[...] + right(a_share)
        rows_of[a_share + 1, share] = sym[...].astype(jnp.bfloat16)
        sent += share_start(a_share + 1)
        row_relay(a_row, w_sent)
        sent += w_sent
        row_finish(a_row)
        second = left(a_row)
        share_finish(a_share + 1)
        total = 3.0 * sym[...] - 2.0 * (second + right(a_share + 1))
        for i in range(per_row):
            keep = keep_row(rpat, row * per_row + i, share_first, share_cols)
            part = slice(i * BLOCK, (i + 1) * BLOCK)
            updated = masked(keep, total[part, :]).astype(jnp.bfloat16)
            if iteration == ITERS - 1:
                out_ref[part, :] = updated
            else:
                rows_of[a_share + 2, share, part, :] = updated
        if iteration == ITERS - 1:
            break
        a_row, a_share = a_row + 1, a_share + 2
        cols_of[a_row, own_rows(row), :] = rows_of[a_share, share]
        x_sent = row_start(a_row)
        sent += share_start(a_share)
        row_relay(a_row, x_sent)
        sent += x_sent
        row_finish(a_row)
        fwd[...] = left(a_row)
        a_row += 1
        cols_of[a_row, own_rows(row), :] = fwd[...].astype(jnp.bfloat16)
        w_sent = row_start(a_row)

    for copy in sent:
        copy.wait_send()


SENDS = 96


def whole_kernel(
    axes,
    nrow,
    ncol,
    nka,
    density_in,
    start_in,
    dpat,
    rpat,
    out_ref,
    d_stage,
    x_stage,
    df,
    xf,
    sym,
    squares,
    sym_b,
    squares_b,
    x1,
    f1,
    strips,
    send,
    drecv,
    xrecv,
    srecv,
    local,
):
    rows, order = density_in.shape
    cols = start_in.shape[1]
    nshare = ncol * nka
    nhi = nrow // LANES
    per_row = rows // BLOCK
    row = lax.axis_index("row")
    col = lax.axis_index("col")
    ka = lax.axis_index("ka")
    mine = col * nka + ka
    core_share = (1 - col) * nka + ka
    y_share = col * nka + (1 - ka)
    diag_share = (1 - col) * nka + (1 - ka)
    hi, lo = row // LANES, row % LANES

    def device(r, c, k):
        where = {"row": r, "col": c, "ka": k}
        return tuple(where[name] for name in axes)

    z_rows = [((hi + d) % nhi) * LANES + lo for d in (1, nhi - 1, *range(2, nhi - 1))]
    x_row = hi * LANES + 1 - lo
    x_rows = [x_row] + [(z // LANES) * LANES + 1 - lo for z in z_rows]
    z_devices = [device(r, col, ka) for r in z_rows]
    x_device = device(x_row, col, ka)
    y_device = device(row, col, 1 - ka)
    core_device = device(row, 1 - col, ka)
    greeted = z_devices + [x_device, y_device, core_device]

    d_copy = pltpu.make_async_copy(density_in, d_stage, local.at[0])
    d_copy.start()
    x_copy = pltpu.make_async_copy(start_in, x_stage, local.at[1])
    x_copy.start()
    barrier = pltpu.get_barrier_semaphore()
    for peer in greeted:
        pl.semaphore_signal(barrier, inc=1, device_id=peer, device_id_type=MESH)

    def block(ref, s, r):
        return ref.at[s, pl.ds(pl.multiple_of(r * rows, rows), rows), :]

    sent = []

    def push(ref, sem, target):
        copy = pltpu.make_async_remote_copy(
            src_ref=ref,
            dst_ref=ref,
            send_sem=send.at[len(sent)],
            recv_sem=sem,
            device_id=target,
            device_id_type=MESH,
        )
        copy.start()
        sent.append(copy)

    def arrived(ref, sem):
        pltpu.make_async_remote_copy(
            src_ref=ref,
            dst_ref=ref,
            send_sem=send.at[0],
            recv_sem=sem,
            device_id=core_device,
            device_id_type=MESH,
        ).wait_recv()

    def push_d(s, r, *targets):
        for target in targets:
            push(block(df, s, r), drecv.at[s, r], target)

    def push_x(s, r, *targets):
        for target in targets:
            push(block(xf, s, r), xrecv.at[s, r], target)

    def wait_d(s, r):
        arrived(block(df, s, r), drecv.at[s, r])

    def wait_x(s, r):
        arrived(block(xf, s, r), xrecv.at[s, r])

    def share_rows(s):
        return pl.ds(pl.multiple_of(s * cols, cols), cols)

    def left_add(total, s, right_ref, lead):
        part = right_ref[(*lead, share_rows(s), slice(None))]
        total[...] += dot(df[s], part)

    def left_parts(s):
        left_add(sym, s, xf, (mine,))
        left_add(squares, s, df, (mine,))

    def right_parts(s):
        sym[...] += dot(xf[s], df[mine, share_rows(s), :])

    own = pl.ds(pl.multiple_of(row * rows, rows), rows)
    first_col = pl.multiple_of(mine * cols, cols)

    d_copy.wait()
    for i in range(per_row):
        keep = keep_row(dpat, row * per_row + i, 0, order)
        kept = masked(keep, d_stage[i * BLOCK : (i + 1) * BLOCK, :]).astype(jnp.bfloat16)
        where = pl.ds(pl.multiple_of(row * rows + i * BLOCK, BLOCK), BLOCK)
        for s in range(nshare):
            df[s, where, :] = kept[:, s * cols : (s + 1) * cols]
    x_copy.wait()
    for b in range(order // BLOCK):
        keep = keep_row(rpat, b, first_col, cols)
        part = slice(b * BLOCK, (b + 1) * BLOCK)
        xf[mine, part, :] = masked(keep, x_stage[part, :]).astype(jnp.bfloat16)
    pl.semaphore_wait(barrier, len(greeted))

    push_x(mine, row, y_device)
    push_d(mine, row, *z_devices, x_device)
    push(xf.at[mine], xrecv.at[mine, 0], core_device)
    sym[...] = jnp.zeros_like(sym)
    squares[...] = jnp.zeros_like(squares)
    wait_x(y_share, row)
    push_x(y_share, row, *z_devices, x_device, core_device)
    for z in z_rows:
        wait_d(mine, z)
        push_d(mine, z, x_device, y_device, core_device)
    for i, z in enumerate(z_rows):
        wait_d(mine, x_rows[i])
        push_d(mine, x_rows[i], y_device, core_device)
        wait_x(y_share, z)
        push_x(y_share, z, x_device, core_device)
    for r in x_rows[nhi - 1 :]:
        wait_d(mine, r)
        push_d(mine, r, y_device, core_device)
    left_parts(mine)
    right_parts(mine)
    arrived(xf.at[core_share], xrecv.at[core_share, 0])
    right_parts(core_share)
    others = z_rows + x_rows
    for i, r in enumerate(others):
        wait_d(y_share, r)
        push_d(y_share, r, core_device)
        if i < nhi:
            wait_x(y_share, x_rows[i])
            push_x(y_share, x_rows[i], core_device)
    right_parts(y_share)
    left_parts(y_share)
    for r in others:
        wait_d(core_share, r)
    left_parts(core_share)
    for r in [row] + others:
        wait_x(diag_share, r)
    right_parts(diag_share)
    for r in others:
        wait_d(diag_share, r)
    left_parts(diag_share)

    sym_b[...] = sym[...].astype(jnp.bfloat16)
    squares_b[...] = squares[...].astype(jnp.bfloat16)
    twice = None
    for s in range(nshare):
        at = slice(s * cols, (s + 1) * cols)
        part = dot(df[s], sym_b[at, :]) + dot(xf[s], squares_b[at, :])
        twice = part if twice is None else twice + part
    sym[...] = 3.0 * sym[...] - 2.0 * twice
    for b in range(order // BLOCK):
        keep = keep_row(rpat, b, first_col, cols)
        part = slice(b * BLOCK, (b + 1) * BLOCK)
        x1[part, :] = masked(keep, sym[part, :]).astype(jnp.bfloat16)

    strips[0, mine] = x1[own, :]

    def push_strip(a, s, *targets):
        for target in targets:
            push(strips.at[a, s], srecv.at[a, s], target)

    push_strip(0, mine, y_device, core_device)

    def density_dot(ref):
        total = None
        for s in range(nshare):
            part = dot(df[s, own, :], ref[s * cols : (s + 1) * cols, :])
            total = part if total is None else total + part
        return total

    forward = density_dot(x1)
    strips[1, mine] = forward.astype(jnp.bfloat16)
    push_strip(1, mine, y_device, core_device)
    full = None
    for s in range(nshare):
        part = dot(df[s], x1[s * cols : (s + 1) * cols, :])
        full = part if full is None else full + part
    f1[...] = full.astype(jnp.bfloat16)
    result = 3.0 * forward - 2.0 * density_dot(f1)
    for a in range(2):
        arrived(strips.at[a, y_share], srecv.at[a, y_share])
        push_strip(a, y_share, core_device)
    for s in (core_share, diag_share):
        for a in range(2):
            arrived(strips.at[a, s], srecv.at[a, s])
    for s in range(nshare):
        at = slice(s * cols, (s + 1) * cols)
        d_part = df[mine, at, :]
        result += 3.0 * dot(strips[0, s], d_part)
        result -= 2.0 * (dot(strips[1, s], d_part) + dot(strips[0, s], squares_b[at, :]))
    for i in range(per_row):
        keep = keep_row(rpat, row * per_row + i, first_col, cols)
        part = slice(i * BLOCK, (i + 1) * BLOCK)
        out_ref[part, :] = masked(keep, result[part, :]).astype(jnp.bfloat16)

    for copy in sent:
        copy.wait_send()


def whole_call(axes, nrow, ncol, nka, rows, order, cols):
    nshare = ncol * nka
    vmem = pl.BlockSpec(memory_space=pltpu.VMEM)
    hbm = pl.BlockSpec(memory_space=pl.ANY)
    bf16, f32 = jnp.bfloat16, jnp.float32
    return pl.pallas_call(
        functools.partial(whole_kernel, axes, nrow, ncol, nka),
        out_shape=jax.ShapeDtypeStruct((rows, cols), bf16),
        in_specs=[hbm, hbm, vmem, vmem],
        out_specs=vmem,
        scratch_shapes=[
            pltpu.VMEM((rows, order), bf16),
            pltpu.VMEM((order, cols), bf16),
            pltpu.VMEM((nshare, order, cols), bf16),
            pltpu.VMEM((nshare, order, cols), bf16),
            pltpu.VMEM((order, cols), f32),
            pltpu.VMEM((order, cols), f32),
            pltpu.VMEM((order, cols), bf16),
            pltpu.VMEM((order, cols), bf16),
            pltpu.VMEM((order, cols), bf16),
            pltpu.VMEM((order, cols), bf16),
            pltpu.VMEM((2, nshare, rows, cols), bf16),
            pltpu.SemaphoreType.DMA((SENDS,)),
            pltpu.SemaphoreType.DMA((nshare, nrow)),
            pltpu.SemaphoreType.DMA((nshare, nrow)),
            pltpu.SemaphoreType.DMA((2, nshare)),
            pltpu.SemaphoreType.DMA((2,)),
        ],
        compiler_params=pltpu.CompilerParams(
            collective_id=1, has_side_effects=True, vmem_limit_bytes=40 * 1024 * 1024
        ),
        cost_estimate=pl.CostEstimate(
            flops=13 * order * order * cols,
            bytes_accessed=2 * order * (rows + cols),
            transcendentals=0,
        ),
    )


def solution(mesh):
    nrow, ncol, nka = (mesh.shape[name] for name in ("row", "col", "ka"))
    nshare = ncol * nka

    def body(density_rows, response_start, density_pattern, response_pattern):
        rows, order = density_rows.shape
        share_cols = response_start.shape[1]
        if ncol == 2 and nka == 2 and nrow == 8 and order <= 1024:
            return whole_call(mesh.axis_names, nrow, ncol, nka, rows, order, share_cols)(
                density_rows, response_start, density_pattern, response_pattern
            )
        row_sends = nrow // LANES - 1 + LANES - 1 + (nrow // LANES - 1) * (LANES - 1)
        vmem = pl.BlockSpec(memory_space=pltpu.VMEM)
        return pl.pallas_call(
            functools.partial(kernel, mesh.axis_names, nrow, ncol, nka),
            out_shape=jax.ShapeDtypeStruct((rows, share_cols), jnp.bfloat16),
            in_specs=[vmem] * 4,
            out_specs=vmem,
            scratch_shapes=[
                pltpu.VMEM((rows, order), jnp.bfloat16),
                pltpu.VMEM((order, share_cols), jnp.bfloat16),
                pltpu.VMEM((rows, share_cols), jnp.float32),
                pltpu.VMEM((rows, share_cols), jnp.float32),
                pltpu.VMEM((2 * ITERS, order, share_cols), jnp.bfloat16),
                pltpu.VMEM((2 * ITERS, nshare, rows, share_cols), jnp.bfloat16),
                pltpu.SemaphoreType.DMA((2 * ITERS, row_sends)),
                pltpu.SemaphoreType.DMA((2 * ITERS, nrow)),
                pltpu.SemaphoreType.DMA((2 * ITERS, nshare)),
                pltpu.SemaphoreType.DMA((2 * ITERS, nshare)),
            ],
            compiler_params=pltpu.CompilerParams(
                collective_id=0, has_side_effects=True, vmem_limit_bytes=40 * 1024 * 1024
            ),
            cost_estimate=pl.CostEstimate(
                flops=8 * ITERS * rows * order * share_cols,
                bytes_accessed=2 * order * (rows + share_cols),
                transcendentals=0,
            ),
        )(density_rows, response_start, density_pattern, response_pattern)

    return jax.shard_map(
        body,
        mesh=mesh,
        in_specs=(P("row", None), P(None, ("col", "ka")), P(), P()),
        out_specs=P("row", ("col", "ka")),
        check_vma=False,
    )
```

```python
import functools

import jax
import jax.numpy as jnp
from jax import lax
from jax.experimental import pallas as pl
from jax.experimental.pallas import tpu as pltpu
from jax.sharding import PartitionSpec as P

BLOCK = 64
ITERS = 2
LANES = 2
MESH = pl.DeviceIdType.MESH


def keep_row(pattern_ref, block_row, first_col, cols):
    listed = pattern_ref[pl.ds(block_row, 1), :]
    col_block = (lax.broadcasted_iota(jnp.int32, (1, cols), 1) + first_col) // BLOCK
    keep = col_block == block_row
    for k in range(listed.shape[1]):
        keep = jnp.logical_or(keep, col_block == listed[:, k : k + 1])
    return keep


def masked(keep, values):
    values = values.astype(jnp.float32)
    return jnp.where(jnp.broadcast_to(keep, values.shape), values, jnp.zeros_like(values))


def dot(a, b):
    return jnp.dot(a, b, preferred_element_type=jnp.float32)


def kernel(
    axes,
    nrow,
    ncol,
    nka,
    density_in,
    start_in,
    dpat,
    rpat,
    out_ref,
    density,
    start,
    fwd,
    sym,
    cols_of,
    rows_of,
    row_send,
    row_recv,
    share_send,
    share_recv,
):
    rows, order = density_in.shape
    share_cols = start_in.shape[1]
    nshare = ncol * nka
    nhi = nrow // LANES
    per_row = rows // BLOCK
    row = lax.axis_index("row")
    col = lax.axis_index("col")
    ka = lax.axis_index("ka")
    share = col * nka + ka
    hi, lo = row // LANES, row % LANES

    def device(r, c, k):
        where = {"row": r, "col": c, "ka": k}
        return tuple(where[name] for name in axes)

    hi_peers = [((hi + d) % nhi) * LANES + lo for d in range(1, nhi)]
    lo_peers = [hi * LANES + (lo + d) % LANES for d in range(1, LANES)]
    share_peers = [(share + d) % nshare for d in range(1, nshare)]

    def own_rows(r):
        return pl.ds(pl.multiple_of(r * rows, rows), rows)

    def row_copy(a, slot, target, sem):
        return pltpu.make_async_remote_copy(
            src_ref=cols_of.at[a, own_rows(slot), :],
            dst_ref=cols_of.at[a, own_rows(slot), :],
            send_sem=row_send.at[a, sem],
            recv_sem=row_recv.at[a, slot],
            device_id=device(target, col, ka),
            device_id_type=MESH,
        )

    def row_start(a):
        started = []
        for i, peer in enumerate(hi_peers + lo_peers):
            copy = row_copy(a, row, peer, i)
            copy.start()
            started.append(copy)
        return started

    def row_relay(a, started):
        sem = len(started)
        for peer in hi_peers:
            row_copy(a, peer, peer, 0).wait_recv()
            for target in lo_peers:
                copy = row_copy(a, peer, target, sem)
                copy.start()
                started.append(copy)
                sem += 1

    def row_finish(a):
        for d in range(nhi):
            for e in range(1, LANES):
                slot = ((hi + d) % nhi) * LANES + (lo + e) % LANES
                row_copy(a, slot, slot, 0).wait_recv()

    def share_copy(a, slot, target, sem):
        return pltpu.make_async_remote_copy(
            src_ref=rows_of.at[a, slot],
            dst_ref=rows_of.at[a, slot],
            send_sem=share_send.at[a, sem],
            recv_sem=share_recv.at[a, slot],
            device_id=device(row, target // nka, target % nka),
            device_id_type=MESH,
        )

    def share_start(a):
        started = []
        for i, peer in enumerate(share_peers):
            copy = share_copy(a, share, peer, i)
            copy.start()
            started.append(copy)
        return started

    def share_finish(a):
        for peer in share_peers:
            share_copy(a, peer, peer, 0).wait_recv()

    def left(a):
        return dot(density[...], cols_of[a])

    def right(a):
        total = None
        for s in range(nshare):
            part = dot(rows_of[a, s], cols_of[0, s * share_cols : (s + 1) * share_cols, :])
            total = part if total is None else total + part
        return total

    barrier = pltpu.get_barrier_semaphore()
    greeted = [device(r, col, ka) for r in hi_peers + lo_peers]
    greeted += [device(row, s // nka, s % nka) for s in share_peers]
    for peer in greeted:
        pl.semaphore_signal(barrier, inc=1, device_id=peer, device_id_type=MESH)

    for i in range(per_row):
        keep = keep_row(dpat, row * per_row + i, 0, order)
        part = slice(i * BLOCK, (i + 1) * BLOCK)
        density[part, :] = masked(keep, density_in[part, :]).astype(jnp.bfloat16)
    share_first = pl.multiple_of(share * share_cols, share_cols)
    cols_of[0, own_rows(row), :] = density[:, pl.ds(share_first, share_cols)]
    pl.semaphore_wait(barrier, len(greeted))
    sent = row_start(0)

    for b in range(order // BLOCK):
        keep = keep_row(rpat, b, share_first, share_cols)
        part = slice(b * BLOCK, (b + 1) * BLOCK)
        start[part, :] = masked(keep, start_in[part, :]).astype(jnp.bfloat16)
    rows_of[0, share] = start[own_rows(row), :]
    sent += share_start(0)
    fwd[...] = dot(density[...], start[...])
    cols_of[1, own_rows(row), :] = fwd[...].astype(jnp.bfloat16)

    d_sent = sent[: nrow // LANES - 1 + LANES - 1]
    relayed = list(d_sent)
    row_relay(0, relayed)
    sent += relayed[len(d_sent) :]
    w_sent = row_start(1)
    row_finish(0)

    a_row, a_share = 1, 0
    for iteration in range(ITERS):
        share_finish(a_share)
        sym[...] = fwd[...] + right(a_share)
        rows_of[a_share + 1, share] = sym[...].astype(jnp.bfloat16)
        sent += share_start(a_share + 1)
        row_relay(a_row, w_sent)
        sent += w_sent
        row_finish(a_row)
        second = left(a_row)
        share_finish(a_share + 1)
        total = 3.0 * sym[...] - 2.0 * (second + right(a_share + 1))
        for i in range(per_row):
            keep = keep_row(rpat, row * per_row + i, share_first, share_cols)
            part = slice(i * BLOCK, (i + 1) * BLOCK)
            updated = masked(keep, total[part, :]).astype(jnp.bfloat16)
            if iteration == ITERS - 1:
                out_ref[part, :] = updated
            else:
                rows_of[a_share + 2, share, part, :] = updated
        if iteration == ITERS - 1:
            break
        a_row, a_share = a_row + 1, a_share + 2
        cols_of[a_row, own_rows(row), :] = rows_of[a_share, share]
        x_sent = row_start(a_row)
        sent += share_start(a_share)
        row_relay(a_row, x_sent)
        sent += x_sent
        row_finish(a_row)
        fwd[...] = left(a_row)
        a_row += 1
        cols_of[a_row, own_rows(row), :] = fwd[...].astype(jnp.bfloat16)
        w_sent = row_start(a_row)

    for copy in sent:
        copy.wait_send()


SENDS = 96


def whole_kernel(
    axes,
    nrow,
    ncol,
    nka,
    density_in,
    start_in,
    dpat,
    rpat,
    out_ref,
    d_stage,
    x_stage,
    df,
    xf,
    sym,
    squares,
    sym_b,
    squares_b,
    x1,
    f1,
    strips,
    send,
    drecv,
    xrecv,
    srecv,
    local,
):
    rows, order = density_in.shape
    cols = start_in.shape[1]
    nshare = ncol * nka
    nhi = nrow // LANES
    per_row = rows // BLOCK
    row = lax.axis_index("row")
    col = lax.axis_index("col")
    ka = lax.axis_index("ka")
    mine = col * nka + ka
    core_share = (1 - col) * nka + ka
    y_share = col * nka + (1 - ka)
    diag_share = (1 - col) * nka + (1 - ka)
    hi, lo = row // LANES, row % LANES

    def device(r, c, k):
        where = {"row": r, "col": c, "ka": k}
        return tuple(where[name] for name in axes)

    z_rows = [((hi + d) % nhi) * LANES + lo for d in (1, nhi - 1, *range(2, nhi - 1))]
    x_row = hi * LANES + 1 - lo
    x_rows = [x_row] + [(z // LANES) * LANES + 1 - lo for z in z_rows]
    z_devices = [device(r, col, ka) for r in z_rows]
    x_device = device(x_row, col, ka)
    y_device = device(row, col, 1 - ka)
    core_device = device(row, 1 - col, ka)
    greeted = z_devices + [x_device, y_device, core_device]

    d_copy = pltpu.make_async_copy(density_in, d_stage, local.at[0])
    d_copy.start()
    x_copy = pltpu.make_async_copy(start_in, x_stage, local.at[1])
    x_copy.start()
    barrier = pltpu.get_barrier_semaphore()
    for peer in greeted:
        pl.semaphore_signal(barrier, inc=1, device_id=peer, device_id_type=MESH)

    def block(ref, s, r):
        return ref.at[s, pl.ds(pl.multiple_of(r * rows, rows), rows), :]

    sent = []

    def push(ref, sem, target):
        copy = pltpu.make_async_remote_copy(
            src_ref=ref,
            dst_ref=ref,
            send_sem=send.at[len(sent)],
            recv_sem=sem,
            device_id=target,
            device_id_type=MESH,
        )
        copy.start()
        sent.append(copy)

    def arrived(ref, sem):
        pltpu.make_async_remote_copy(
            src_ref=ref,
            dst_ref=ref,
            send_sem=send.at[0],
            recv_sem=sem,
            device_id=core_device,
            device_id_type=MESH,
        ).wait_recv()

    def push_d(s, r, *targets):
        for target in targets:
            push(block(df, s, r), drecv.at[s, r], target)

    def push_x(s, r, *targets):
        for target in targets:
            push(block(xf, s, r), xrecv.at[s, r], target)

    def wait_d(s, r):
        arrived(block(df, s, r), drecv.at[s, r])

    def wait_x(s, r):
        arrived(block(xf, s, r), xrecv.at[s, r])

    def share_rows(s):
        return pl.ds(pl.multiple_of(s * cols, cols), cols)

    def left_add(total, s, right_ref, lead):
        part = right_ref[(*lead, share_rows(s), slice(None))]
        total[...] += dot(df[s], part)

    def left_parts(s):
        left_add(sym, s, xf, (mine,))
        left_add(squares, s, df, (mine,))

    def right_parts(s):
        sym[...] += dot(xf[s], df[mine, share_rows(s), :])

    own = pl.ds(pl.multiple_of(row * rows, rows), rows)
    first_col = pl.multiple_of(mine * cols, cols)

    d_copy.wait()
    for i in range(per_row):
        keep = keep_row(dpat, row * per_row + i, 0, order)
        kept = masked(keep, d_stage[i * BLOCK : (i + 1) * BLOCK, :]).astype(jnp.bfloat16)
        where = pl.ds(pl.multiple_of(row * rows + i * BLOCK, BLOCK), BLOCK)
        for s in range(nshare):
            df[s, where, :] = kept[:, s * cols : (s + 1) * cols]
    x_copy.wait()
    for b in range(order // BLOCK):
        keep = keep_row(rpat, b, first_col, cols)
        part = slice(b * BLOCK, (b + 1) * BLOCK)
        xf[mine, part, :] = masked(keep, x_stage[part, :]).astype(jnp.bfloat16)
    pl.semaphore_wait(barrier, len(greeted))

    push_x(mine, row, y_device)
    push_d(mine, row, *z_devices, x_device)
    push(xf.at[mine], xrecv.at[mine, 0], core_device)
    sym[...] = jnp.zeros_like(sym)
    squares[...] = jnp.zeros_like(squares)
    wait_x(y_share, row)
    push_x(y_share, row, *z_devices, x_device, core_device)
    for z in z_rows:
        wait_d(mine, z)
        push_d(mine, z, x_device, y_device, core_device)
    for i, z in enumerate(z_rows):
        wait_d(mine, x_rows[i])
        push_d(mine, x_rows[i], y_device, core_device)
        wait_x(y_share, z)
        push_x(y_share, z, x_device, core_device)
    for r in x_rows[nhi - 1 :]:
        wait_d(mine, r)
        push_d(mine, r, y_device, core_device)
    left_parts(mine)
    right_parts(mine)
    arrived(xf.at[core_share], xrecv.at[core_share, 0])
    right_parts(core_share)
    others = z_rows + x_rows
    for r in others:
        wait_d(core_share, r)
    left_parts(core_share)
    for i, r in enumerate(others):
        wait_d(y_share, r)
        push_d(y_share, r, core_device)
        if i < nhi:
            wait_x(y_share, x_rows[i])
            push_x(y_share, x_rows[i], core_device)
    right_parts(y_share)
    left_parts(y_share)
    for r in [row] + others:
        wait_x(diag_share, r)
    right_parts(diag_share)
    for r in others:
        wait_d(diag_share, r)
    left_parts(diag_share)

    sym_b[...] = sym[...].astype(jnp.bfloat16)
    squares_b[...] = squares[...].astype(jnp.bfloat16)
    twice = None
    for s in range(nshare):
        at = slice(s * cols, (s + 1) * cols)
        part = dot(df[s], sym_b[at, :]) + dot(xf[s], squares_b[at, :])
        twice = part if twice is None else twice + part
    sym[...] = 3.0 * sym[...] - 2.0 * twice
    for b in range(order // BLOCK):
        keep = keep_row(rpat, b, first_col, cols)
        part = slice(b * BLOCK, (b + 1) * BLOCK)
        x1[part, :] = masked(keep, sym[part, :]).astype(jnp.bfloat16)

    strips[0, mine] = x1[own, :]

    def push_strip(a, s, *targets):
        for target in targets:
            push(strips.at[a, s], srecv.at[a, s], target)

    push_strip(0, mine, y_device, core_device)

    def density_dot(ref):
        total = None
        for s in range(nshare):
            part = dot(df[s, own, :], ref[s * cols : (s + 1) * cols, :])
            total = part if total is None else total + part
        return total

    forward = density_dot(x1)
    strips[1, mine] = forward.astype(jnp.bfloat16)
    push_strip(1, mine, y_device, core_device)
    full = None
    for s in range(nshare):
        part = dot(df[s], x1[s * cols : (s + 1) * cols, :])
        full = part if full is None else full + part
    f1[...] = full.astype(jnp.bfloat16)
    result = 3.0 * forward - 2.0 * density_dot(f1)
    def share_terms(s):
        at = share_rows(s)
        d_part = df[mine, at, :]
        start_part = dot(strips[0, s], d_part)
        rest = dot(strips[1, s], d_part) + dot(strips[0, s], squares_b[at, :])
        return 3.0 * start_part - 2.0 * rest

    result += share_terms(mine)
    for a in range(2):
        arrived(strips.at[a, core_share], srecv.at[a, core_share])
    result += share_terms(core_share)
    for s, targets in ((y_share, (core_device,)), (diag_share, ())):
        for a in range(2):
            arrived(strips.at[a, s], srecv.at[a, s])
            push_strip(a, s, *targets)
        result += share_terms(s)
    for i in range(per_row):
        keep = keep_row(rpat, row * per_row + i, first_col, cols)
        part = slice(i * BLOCK, (i + 1) * BLOCK)
        out_ref[part, :] = masked(keep, result[part, :]).astype(jnp.bfloat16)

    for copy in sent:
        copy.wait_send()


def whole_call(axes, nrow, ncol, nka, rows, order, cols):
    nshare = ncol * nka
    vmem = pl.BlockSpec(memory_space=pltpu.VMEM)
    hbm = pl.BlockSpec(memory_space=pl.ANY)
    bf16, f32 = jnp.bfloat16, jnp.float32
    return pl.pallas_call(
        functools.partial(whole_kernel, axes, nrow, ncol, nka),
        out_shape=jax.ShapeDtypeStruct((rows, cols), bf16),
        in_specs=[hbm, hbm, vmem, vmem],
        out_specs=vmem,
        scratch_shapes=[
            pltpu.VMEM((rows, order), bf16),
            pltpu.VMEM((order, cols), bf16),
            pltpu.VMEM((nshare, order, cols), bf16),
            pltpu.VMEM((nshare, order, cols), bf16),
            pltpu.VMEM((order, cols), f32),
            pltpu.VMEM((order, cols), f32),
            pltpu.VMEM((order, cols), bf16),
            pltpu.VMEM((order, cols), bf16),
            pltpu.VMEM((order, cols), bf16),
            pltpu.VMEM((order, cols), bf16),
            pltpu.VMEM((2, nshare, rows, cols), bf16),
            pltpu.SemaphoreType.DMA((SENDS,)),
            pltpu.SemaphoreType.DMA((nshare, nrow)),
            pltpu.SemaphoreType.DMA((nshare, nrow)),
            pltpu.SemaphoreType.DMA((2, nshare)),
            pltpu.SemaphoreType.DMA((2,)),
        ],
        compiler_params=pltpu.CompilerParams(
            collective_id=1, has_side_effects=True, vmem_limit_bytes=40 * 1024 * 1024
        ),
        cost_estimate=pl.CostEstimate(
            flops=13 * order * order * cols,
            bytes_accessed=2 * order * (rows + cols),
            transcendentals=0,
        ),
    )


def solution(mesh):
    nrow, ncol, nka = (mesh.shape[name] for name in ("row", "col", "ka"))
    nshare = ncol * nka

    def body(density_rows, response_start, density_pattern, response_pattern):
        rows, order = density_rows.shape
        share_cols = response_start.shape[1]
        if ncol == 2 and nka == 2 and nrow == 8 and order <= 1024:
            return whole_call(mesh.axis_names, nrow, ncol, nka, rows, order, share_cols)(
                density_rows, response_start, density_pattern, response_pattern
            )
        row_sends = nrow // LANES - 1 + LANES - 1 + (nrow // LANES - 1) * (LANES - 1)
        vmem = pl.BlockSpec(memory_space=pltpu.VMEM)
        return pl.pallas_call(
            functools.partial(kernel, mesh.axis_names, nrow, ncol, nka),
            out_shape=jax.ShapeDtypeStruct((rows, share_cols), jnp.bfloat16),
            in_specs=[vmem] * 4,
            out_specs=vmem,
            scratch_shapes=[
                pltpu.VMEM((rows, order), jnp.bfloat16),
                pltpu.VMEM((order, share_cols), jnp.bfloat16),
                pltpu.VMEM((rows, share_cols), jnp.float32),
                pltpu.VMEM((rows, share_cols), jnp.float32),
                pltpu.VMEM((2 * ITERS, order, share_cols), jnp.bfloat16),
                pltpu.VMEM((2 * ITERS, nshare, rows, share_cols), jnp.bfloat16),
                pltpu.SemaphoreType.DMA((2 * ITERS, row_sends)),
                pltpu.SemaphoreType.DMA((2 * ITERS, nrow)),
                pltpu.SemaphoreType.DMA((2 * ITERS, nshare)),
                pltpu.SemaphoreType.DMA((2 * ITERS, nshare)),
            ],
            compiler_params=pltpu.CompilerParams(
                collective_id=0, has_side_effects=True, vmem_limit_bytes=40 * 1024 * 1024
            ),
            cost_estimate=pl.CostEstimate(
                flops=8 * ITERS * rows * order * share_cols,
                bytes_accessed=2 * order * (rows + share_cols),
                transcendentals=0,
            ),
        )(density_rows, response_start, density_pattern, response_pattern)

    return jax.shard_map(
        body,
        mesh=mesh,
        in_specs=(P("row", None), P(None, ("col", "ka")), P(), P()),
        out_specs=P("row", ("col", "ka")),
        check_vma=False,
    )
```
